512 devices in a mesh: frame: 8 (over z_hi, core), patch: 32 (over x, y), tp: 2 (over z_lo).
Axes of the slice: x: 4, y: 8, z: 8 (z_hi: 4, z_lo: 2; z = z_hi * 2 + z_lo), core: 2. Of those that a mesh axis runs over, the one named last changes fastest.
Arguments:
- residual_codes: int32 [16, 64, 32, 1536], P('frame', 'patch', None, 'tp'), may hold values from -127 to 127
- exponents: int32 [16, 64, 32, 24], P('frame', 'patch', None, 'tp'), may hold values from -8 to -4
- conv_weight: bfloat16 [3, 3, 3, 1536], replicated, may hold values from -1.25 to 1.25
- timestep: int32 [16], P('frame'), may hold values from 0 to 49
- modulation: bfloat16 [50, 2, 1536], replicated, may hold values from -3 to 3
- query_weight: bfloat16 [1536, 768], P(None, 'tp'), as said below
- key_weight: bfloat16 [1536, 768], P(None, 'tp'), as said below
- value_weight: bfloat16 [1536, 768], P(None, 'tp'), may hold values from -0.15625 to 0.15625
Outputs:
- attended: bfloat16 [16, 64, 32, 768], P('frame', 'patch', None, 'tp')
The draws below stay inside these ranges and needn't reach their ends.
Inputs may be any that keep to these rules, and one draw needn't show every extreme that they name: `query_weight`: entries of order D ** -0.5. `key_weight`: entries of order D ** -0.5.
All inputs are finite; a program needn't handle non-finite values.
Results may differ from the reference program's by a relative error of at most 0.02.
The reference program's roundings to bfloat16 on the way count: a program that leaves them out, or rounds other values in their place, can miss the bound.
Values may be sent and summed in bfloat16 or wider, within the bound.
No kernel may reach another device: no remote copies, remote signals or barrier semaphores. Data moves between devices by JAX's collectives and lax.ppermute only.
A program may use at most 128 MiB of HBM per device.

```python
import math
import jax
import jax.numpy as jnp
from jax import lax

D = 1536
HEADS = 12
HEAD_DIM = 64
BLOCK = 64
STEPS = 50
F_DEV = 2
WW = 32
FR = 16
HH = 64
N_FRAME = 8


def projection(key):
    base = jax.random.normal(key, (D, HEADS * HEAD_DIM), jnp.float32) / math.sqrt(D)
    return base


def draw_query_weight(key, part):
    key = jax.random.fold_in(key, 11)
    matrix = projection(key)
    return matrix.astype(jnp.bfloat16)


def draw_key_weight(key, part):
    key = jax.random.fold_in(key, 23)
    matrix = projection(key)
    return matrix.astype(jnp.bfloat16)


def set_ends(values, key, least, top_value):
    shape = values.shape
    place = [jax.random.randint(jax.random.fold_in(key, axis), (), 0, shape[axis]) for axis in range(len(shape))]
    values = values.at[tuple(place)].set(least)
    longest = shape.index(max(shape))
    place[longest] = (place[longest] + 1) % shape[longest]
    return values.at[tuple(place)].set(top_value)


def level_of(own_key, dims, pieces, smallest, high):
    level, own = 1.0, jax.random.fold_in(own_key, 6)
    for position, blocks in pieces:
        steps = jnp.exp(jax.random.uniform(jax.random.fold_in(own, position), (blocks,), jnp.float32, smallest / len(pieces), high / len(pieces)))
        level = level * jnp.repeat(steps, dims[position] // blocks).reshape([-1 if axis == position else 1 for axis in range(len(dims))])
    return level


def centred(key, extent, width, limit, cuts=(), kind=jnp.bfloat16):
    entries = width * jax.random.normal(key, extent, jnp.float32)
    if cuts:
        entries = entries * level_of(key, extent, cuts, -0.22, 0.18)
    return jnp.clip(entries, -limit, limit).astype(kind)


def setup_inputs(seed: int = 0) -> dict:
    key_of = jax.random.split(jax.random.key(seed), 9)
    residual_codes = set_ends(jax.random.randint(key_of[0], (FR, HH, WW, D), -127, 128), jax.random.fold_in(key_of[0], 1), -127, 127).astype(jnp.int32)
    exponents = set_ends(jax.random.randint(key_of[1], (FR, HH, WW, D // BLOCK), -8, -3), jax.random.fold_in(key_of[1], 1), -8, (-3) - 1).astype(jnp.int32)
    conv_weight = centred(key_of[2], (3, 3, 3, D), 27 ** -0.5, 1.25)
    timestep = set_ends(jax.random.randint(key_of[3], (FR,), 0, STEPS), jax.random.fold_in(key_of[3], 1), 0, STEPS - 1).astype(jnp.int32)
    modulation = centred(key_of[4], (STEPS, 2, D), 0.5, 3.0)
    query_weight = draw_query_weight(jax.random.fold_in(key_of[8], 71), 0)
    key_weight = draw_key_weight(jax.random.fold_in(key_of[8], 71), 0)
    value_weight = centred(key_of[7], (D, HEADS * HEAD_DIM), D ** -0.5, 0.15625, ((1, 2),))
    return {"residual_codes": residual_codes, "exponents": exponents, "conv_weight": conv_weight, "timestep": timestep, "modulation": modulation, "query_weight": query_weight, "key_weight": key_weight, "value_weight": value_weight}


def dequantize(residual_codes, exponents):
    groups = exponents.shape[-1]
    model_width = residual_codes.shape[-1]
    factor = jnp.exp2(exponents.astype(jnp.float32))
    values = residual_codes.astype(jnp.float32).reshape(residual_codes.shape[:-1] + (groups, model_width // groups))
    return (values * factor[..., None]).reshape(residual_codes.shape)

def convolve(padded, kernel, out_shape):
    frames, tile_rows, tile_cols = out_shape
    result = jnp.zeros(out_shape + (kernel.shape[-1],), jnp.float32)
    for shift_f in range(3):
        for shift_h in range(3):
            for shift_w in range(3):
                window = padded[shift_f:shift_f + frames, shift_h:shift_h + tile_rows, shift_w:shift_w + tile_cols, :]
                result = result + window.astype(jnp.float32) * kernel[shift_f, shift_h, shift_w].astype(jnp.float32)
    return result

def modulate(mixed, modulation, timestep):
    selector = (jnp.arange(modulation.shape[0], dtype=jnp.int32)[None, :] == timestep[:, None]).astype(jnp.float32)
    picked = jnp.einsum('fs,sjd->fjd', selector, modulation.astype(jnp.float32))
    shift_rows = picked[:, 0][:, None, None, :]
    scale_rows = picked[:, 1][:, None, None, :]
    values = mixed.astype(jnp.float32)
    average = lax.optimization_barrier(jnp.mean(values, axis=-1, keepdims=True))
    centered = values - average
    variance = lax.optimization_barrier(jnp.mean(centered * centered, axis=-1, keepdims=True))
    normed = centered / jnp.sqrt(variance + 1e-06) * (1.0 + scale_rows) + shift_rows
    return normed.astype(jnp.bfloat16)

def reference(residual_codes, exponents, conv_weight, timestep, modulation, query_weight, key_weight, value_weight):
    inputs = dequantize(residual_codes, exponents)
    padded = jnp.pad(inputs.astype(jnp.bfloat16), ((1, 1), (1, 1), (1, 1), (0, 0)))
    mixed = (inputs + convolve(padded, conv_weight, (FR, HH, WW))).astype(jnp.bfloat16)
    normed = modulate(mixed, modulation, timestep).reshape(FR * HH * WW, D)
    queries = jnp.dot(normed, query_weight, preferred_element_type=jnp.float32).astype(jnp.bfloat16)
    key_rows = jnp.dot(normed, key_weight, preferred_element_type=jnp.float32).astype(jnp.bfloat16)
    value_rows = jnp.dot(normed, value_weight, preferred_element_type=jnp.float32).astype(jnp.bfloat16)
    stretch_len = F_DEV * HH * WW

    def heads_major(matrix):
        shaped = matrix.reshape(N_FRAME, stretch_len, HEADS, HEAD_DIM).transpose(0, 2, 1, 3)
        return shaped.reshape(N_FRAME * HEADS, stretch_len, HEAD_DIM)

    def attend(triple):
        query_part, key_part, value_part = triple
        scores = jnp.dot(query_part, key_part.T, preferred_element_type=jnp.float32) * HEAD_DIM ** (-0.5)
        row_max = lax.optimization_barrier(jnp.max(scores, axis=1, keepdims=True))
        exps = jnp.exp(scores - row_max)
        totals = lax.optimization_barrier(jnp.sum(exps, axis=1, keepdims=True))
        summed = jnp.dot(exps.astype(jnp.bfloat16), value_part, preferred_element_type=jnp.float32)
        return (summed / totals).astype(jnp.bfloat16)
    outputs = lax.map(attend, (heads_major(queries), heads_major(key_rows), heads_major(value_rows)))
    outputs = outputs.reshape(N_FRAME, HEADS, stretch_len, HEAD_DIM).transpose(0, 2, 1, 3)
    return outputs.reshape(FR, HH, WW, HEADS * HEAD_DIM)
```

```python
import functools

import jax
import jax.numpy as jnp
from jax import lax
from jax.experimental import pallas as pl
from jax.experimental.pallas import tpu as pltpu
from jax.sharding import PartitionSpec as P

HEAD_DIM = 64
LANES = 128
ROWS = 4
COLS = 8
LOG2E = 1.4426950408889634
X_GROUPS = [[x * COLS + y for x in range(ROWS)] for y in range(COLS)]
Y_GROUPS = [[x * COLS + y for y in range(COLS)] for x in range(ROWS)]


def extended(x, sides, width):
    for axis, dim in sides:
        size, length = (lax.axis_size(axis), x.shape[dim])
        up = [(i, (i + 1) % size) for i in range(size - 1)]
        down = [(j, i) for i, j in up]
        last = lax.slice_in_dim(x, length - width, length, axis=dim)
        first = lax.slice_in_dim(x, 0, width, axis=dim)
        before = lax.ppermute(last, axis, up)
        after = lax.ppermute(first, axis, down)
        x = jnp.concatenate([before, x, after], axis=dim)
    return x


def dequantize(residual_codes, exponents):
    groups = exponents.shape[-1]
    channels = residual_codes.shape[-1]
    factor = jnp.exp2(exponents.astype(jnp.float32))
    values = residual_codes.astype(jnp.float32).reshape(
        residual_codes.shape[:-1] + (groups, channels // groups)
    )
    return (values * factor[..., None]).reshape(residual_codes.shape)


def convolve(padded, kernel, out_shape):
    frames, tile_rows, tile_cols = out_shape
    widened = jnp.pad(padded, ((0, 0), (0, 0), (1, 1), (0, 0)))
    result = jnp.zeros(out_shape + (kernel.shape[-1],), jnp.float32)
    for shift_f in range(3):
        for shift_h in range(3):
            for shift_w in range(3):
                window = widened[
                    shift_f : shift_f + frames,
                    shift_h : shift_h + tile_rows,
                    shift_w : shift_w + tile_cols,
                    :,
                ]
                result = result + window.astype(jnp.float32) * kernel[
                    shift_f, shift_h, shift_w
                ].astype(jnp.float32)
    return result


def low_lanes(shape):
    return lax.broadcasted_iota(jnp.int32, shape, len(shape) - 1) < HEAD_DIM


def swap(x):
    return pltpu.roll(x, HEAD_DIM, x.ndim - 1)


def project_kernel(mixed_ref, shift_ref, scale_ref, wq_ref, wk_ref, wv_ref, out_ref):
    half = mixed_ref.shape[1] // 2
    parts = []
    for f in range(2):
        rows = pl.ds(f * half, half)
        x = jnp.concatenate([mixed_ref[0, rows, :], mixed_ref[1, rows, :]], axis=1)
        x = x.astype(jnp.float32)
        average = jnp.mean(x, axis=1, keepdims=True)
        centered = x - average
        variance = jnp.mean(centered * centered, axis=1, keepdims=True)
        x = centered * lax.rsqrt(variance + 1e-06)
        x = x * (1.0 + scale_ref[f : f + 1, :]) + shift_ref[f : f + 1, :]
        parts.append(x.astype(jnp.bfloat16))
    normed = jnp.concatenate(parts, axis=0)
    tokens = 2 * half
    low_all, low_half = low_lanes((tokens, LANES)), low_lanes((half, LANES))
    q, k, v = [
        jnp.dot(normed, w[...], preferred_element_type=jnp.float32)
        for w in (wq_ref, wk_ref, wv_ref)
    ]
    heads = wq_ref.shape[1] // HEAD_DIM
    for pair in range(heads // 2):
        lanes = slice(pair * LANES, (pair + 1) * LANES)
        qp, kp, vp = q[:, lanes], k[:, lanes], v[:, lanes]
        first, second = qp[:half], qp[half:]
        even, odd = 2 * pair, 2 * pair + 1
        out_ref[even, :tokens, :] = jnp.where(low_all, kp, swap(vp)).astype(jnp.bfloat16)
        out_ref[odd, :tokens, :] = jnp.where(low_all, swap(kp), vp).astype(jnp.bfloat16)
        out_ref[even, tokens:, :] = jnp.where(low_half, first, swap(second)).astype(jnp.bfloat16)
        out_ref[odd, tokens:, :] = jnp.where(low_half, swap(first), second).astype(jnp.bfloat16)
    for slot in range(heads, out_ref.shape[0]):
        out_ref[slot] = jnp.zeros(out_ref.shape[1:], jnp.bfloat16)


def attend_kernel(q_ref, kv_ref, out_ref):
    kv = kv_ref[...]
    keys = kv.shape[0]
    ones_v = jnp.where(low_lanes((keys, LANES)), jnp.ones_like(kv), kv)
    slots, half, _ = q_ref.shape
    step = 2
    rows = step * half
    low = low_lanes((rows, LANES))
    factor = LOG2E * HEAD_DIM ** (-0.5)
    for i in range(0, slots, step):
        packed = q_ref[i : i + step].reshape(rows, LANES).astype(jnp.float32)
        first = jnp.where(low, packed, 0.0)
        second = jnp.where(low, swap(packed), 0.0)
        queries = jnp.concatenate([first, second], axis=0).astype(jnp.bfloat16)
        scores = lax.dot_general(
            queries, kv, (((1,), (1,)), ((), ())), preferred_element_type=jnp.float32
        )
        top = jnp.max(scores, axis=1, keepdims=True)
        weights = jnp.exp2((scores - top) * factor).astype(jnp.bfloat16)
        summed = jnp.dot(weights, ones_v, preferred_element_type=jnp.float32)
        done = summed / swap(summed)
        result = jnp.where(low, swap(done[:rows]), done[rows:])
        out_ref[i : i + step] = result.astype(jnp.bfloat16).reshape(step, half, LANES)


def unpack_kernel(in_ref, out_ref):
    half = in_ref.shape[1]
    low = low_lanes((half, LANES))
    for pair in range(out_ref.shape[2] // LANES):
        lanes = slice(pair * LANES, (pair + 1) * LANES)
        even = in_ref[2 * pair].astype(jnp.float32)
        odd = in_ref[2 * pair + 1].astype(jnp.float32)
        out_ref[0, :, lanes] = jnp.where(low, even, swap(odd)).astype(jnp.bfloat16)
        out_ref[1, :, lanes] = jnp.where(low, swap(even), odd).astype(jnp.bfloat16)


def call(kernel, shape, *args):
    return pl.pallas_call(
        kernel,
        out_shape=jax.ShapeDtypeStruct(shape, jnp.bfloat16),
        in_specs=[pl.BlockSpec(memory_space=pltpu.VMEM)] * len(args),
        out_specs=pl.BlockSpec(memory_space=pltpu.VMEM),
        compiler_params=pltpu.CompilerParams(vmem_limit_bytes=48 * 1024 * 1024),
    )(*args)


def local(
    residual_codes,
    exponents,
    conv_weight,
    timestep,
    modulation,
    query_weight,
    key_weight,
    value_weight,
):
    frames, tile_rows, tile_cols, channels = residual_codes.shape
    local_width = query_weight.shape[1]
    tokens = frames * tile_rows * tile_cols
    half = tokens // 2
    grid_shape = (frames, tile_rows, tile_cols)
    inputs_exact = dequantize(residual_codes, exponents)
    inputs_narrow = inputs_exact.astype(jnp.bfloat16)
    pair_index = lax.axis_index("tp")
    kernel = lax.dynamic_slice_in_dim(conv_weight, pair_index * channels, channels, 3)
    padded = extended(inputs_narrow, (("frame", 0), ("patch", 1)), 1)
    mixed_half = (inputs_exact + convolve(padded, kernel, grid_shape)).astype(jnp.bfloat16)
    mixed = lax.all_gather(mixed_half.reshape(tokens, channels), "tp", axis=0)
    picked = jnp.take(modulation, timestep, axis=0).astype(jnp.float32)
    send = call(
        project_kernel,
        (COLS, tokens + half, LANES),
        mixed,
        picked[:, 0],
        picked[:, 1],
        query_weight,
        key_weight,
        value_weight,
    )
    held = lax.all_to_all(send, "patch", 0, 0, axis_index_groups=Y_GROUPS)
    kv = lax.all_gather(held[:, :tokens], "patch", axis_index_groups=X_GROUPS, axis=0)
    result = call(
        attend_kernel,
        (COLS, half, LANES),
        held[:, tokens:],
        kv.reshape(ROWS * COLS * tokens, LANES),
    )
    back = lax.all_to_all(result, "patch", 0, 0, axis_index_groups=Y_GROUPS)
    out = call(unpack_kernel, (frames, half, local_width), back)
    return out.reshape(frames, tile_rows, tile_cols, local_width)


def solution(mesh):
    in_specs = (
        P("frame", "patch", None, "tp"),
        P("frame", "patch", None, "tp"),
        P(),
        P("frame"),
        P(),
        P(None, "tp"),
        P(None, "tp"),
        P(None, "tp"),
    )
    out_specs = P("frame", "patch", None, "tp")
    return jax.shard_map(local, mesh=mesh, in_specs=in_specs, out_specs=out_specs, check_vma=False)
```

```python
import functools

import jax
import jax.numpy as jnp
from jax import lax
from jax.experimental import pallas as pl
from jax.experimental.pallas import tpu as pltpu
from jax.sharding import PartitionSpec as P

HEAD_DIM = 64
LANES = 128
ROWS = 4
COLS = 8
LOG2E = 1.4426950408889634
X_GROUPS = [[x * COLS + y for x in range(ROWS)] for y in range(COLS)]
Y_GROUPS = [[x * COLS + y for y in range(COLS)] for x in range(ROWS)]


def extended(x, sides, width):
    for axis, dim in sides:
        size, length = (lax.axis_size(axis), x.shape[dim])
        up = [(i, (i + 1) % size) for i in range(size - 1)]
        down = [(j, i) for i, j in up]
        last = lax.slice_in_dim(x, length - width, length, axis=dim)
        first = lax.slice_in_dim(x, 0, width, axis=dim)
        before = lax.ppermute(last, axis, up)
        after = lax.ppermute(first, axis, down)
        x = jnp.concatenate([before, x, after], axis=dim)
    return x


def dequantize(residual_codes, exponents):
    groups = exponents.shape[-1]
    channels = residual_codes.shape[-1]
    factor = jnp.exp2(exponents.astype(jnp.float32))
    values = residual_codes.astype(jnp.float32).reshape(
        residual_codes.shape[:-1] + (groups, channels // groups)
    )
    return (values * factor[..., None]).reshape(residual_codes.shape)


def convolve(padded, kernel, out_shape):
    frames, tile_rows, tile_cols = out_shape
    widened = jnp.pad(padded, ((0, 0), (0, 0), (1, 1), (0, 0)))
    result = jnp.zeros(out_shape + (kernel.shape[-1],), jnp.float32)
    for shift_f in range(3):
        for shift_h in range(3):
            for shift_w in range(3):
                window = widened[
                    shift_f : shift_f + frames,
                    shift_h : shift_h + tile_rows,
                    shift_w : shift_w + tile_cols,
                    :,
                ]
                result = result + window.astype(jnp.float32) * kernel[
                    shift_f, shift_h, shift_w
                ].astype(jnp.float32)
    return result


def low_lanes(shape):
    return lax.broadcasted_iota(jnp.int32, shape, len(shape) - 1) < HEAD_DIM


def swap(x):
    return pltpu.roll(x, HEAD_DIM, x.ndim - 1)


def project_kernel(mixed_ref, shift_ref, scale_ref, wq_ref, wk_ref, wv_ref, out_ref):
    half = mixed_ref.shape[1] // 2
    parts = []
    for f in range(2):
        rows = pl.ds(f * half, half)
        x = jnp.concatenate([mixed_ref[0, rows, :], mixed_ref[1, rows, :]], axis=1)
        x = x.astype(jnp.float32)
        average = jnp.mean(x, axis=1, keepdims=True)
        centered = x - average
        variance = jnp.mean(centered * centered, axis=1, keepdims=True)
        x = centered * lax.rsqrt(variance + 1e-06)
        x = x * (1.0 + scale_ref[f : f + 1, :]) + shift_ref[f : f + 1, :]
        parts.append(x.astype(jnp.bfloat16))
    normed = jnp.concatenate(parts, axis=0)
    tokens = 2 * half
    low_all, low_half = low_lanes((tokens, LANES)), low_lanes((half, LANES))
    q, k, v = [
        jnp.dot(normed, w[...], preferred_element_type=jnp.float32)
        for w in (wq_ref, wk_ref, wv_ref)
    ]
    heads = wq_ref.shape[1] // HEAD_DIM
    for pair in range(heads // 2):
        lanes = slice(pair * LANES, (pair + 1) * LANES)
        qp, kp, vp = q[:, lanes], k[:, lanes], v[:, lanes]
        first, second = qp[:half], qp[half:]
        even, odd = 2 * pair, 2 * pair + 1
        out_ref[even, :tokens, :] = jnp.where(low_all, kp, swap(vp)).astype(jnp.bfloat16)
        out_ref[odd, :tokens, :] = jnp.where(low_all, swap(kp), vp).astype(jnp.bfloat16)
        out_ref[even, tokens:, :] = jnp.where(low_half, first, swap(second)).astype(jnp.bfloat16)
        out_ref[odd, tokens:, :] = jnp.where(low_half, swap(first), second).astype(jnp.bfloat16)
    for slot in range(heads, out_ref.shape[0]):
        out_ref[slot] = jnp.zeros(out_ref.shape[1:], jnp.bfloat16)


def attend_kernel(q_ref, kv_ref, out_ref):
    kv = kv_ref[...]
    keys = kv.shape[0]
    ones_v = jnp.where(low_lanes((keys, LANES)), jnp.ones_like(kv), kv)
    slots, half, _ = q_ref.shape
    step = 2
    rows = step * half
    low = low_lanes((rows, LANES))
    factor = LOG2E * HEAD_DIM ** (-0.5)
    for i in range(0, slots, step):
        packed = q_ref[i : i + step].reshape(rows, LANES).astype(jnp.float32)
        first = jnp.where(low, packed, 0.0)
        second = jnp.where(low, swap(packed), 0.0)
        queries = jnp.concatenate([first, second], axis=0).astype(jnp.bfloat16)
        scores = lax.dot_general(
            queries, kv, (((1,), (1,)), ((), ())), preferred_element_type=jnp.float32
        )
        top = jnp.max(scores, axis=1, keepdims=True)
        weights = jnp.exp2((scores - top) * factor).astype(jnp.bfloat16)
        summed = jnp.dot(weights, ones_v, preferred_element_type=jnp.float32)
        done = summed / swap(summed)
        result = jnp.where(low, swap(done[:rows]), done[rows:])
        out_ref[i : i + step] = result.astype(jnp.bfloat16).reshape(step, half, LANES)


def unpack_kernel(in_ref, out_ref):
    half = in_ref.shape[1]
    low = low_lanes((half, LANES))
    for pair in range(out_ref.shape[2] // LANES):
        lanes = slice(pair * LANES, (pair + 1) * LANES)
        even = in_ref[2 * pair].astype(jnp.float32)
        odd = in_ref[2 * pair + 1].astype(jnp.float32)
        out_ref[0, :, lanes] = jnp.where(low, even, swap(odd)).astype(jnp.bfloat16)
        out_ref[1, :, lanes] = jnp.where(low, swap(even), odd).astype(jnp.bfloat16)


def call(kernel, shape, *args):
    return pl.pallas_call(
        kernel,
        out_shape=jax.ShapeDtypeStruct(shape, jnp.bfloat16),
        in_specs=[pl.BlockSpec(memory_space=pltpu.VMEM)] * len(args),
        out_specs=pl.BlockSpec(memory_space=pltpu.VMEM),
        compiler_params=pltpu.CompilerParams(vmem_limit_bytes=48 * 1024 * 1024),
    )(*args)


def local(
    residual_codes,
    exponents,
    conv_weight,
    timestep,
    modulation,
    query_weight,
    key_weight,
    value_weight,
):
    frames, tile_rows, tile_cols, channels = residual_codes.shape
    local_width = query_weight.shape[1]
    tokens = frames * tile_rows * tile_cols
    half = tokens // 2
    grid_shape = (frames, tile_rows, tile_cols)
    inputs_exact = dequantize(residual_codes, exponents)
    inputs_narrow = inputs_exact.astype(jnp.bfloat16)
    pair_index = lax.axis_index("tp")
    kernel = lax.dynamic_slice_in_dim(conv_weight, pair_index * channels, channels, 3)
    padded = extended(inputs_narrow, (("frame", 0), ("patch", 1)), 1)
    mixed_half = (inputs_exact + convolve(padded, kernel, grid_shape)).astype(jnp.bfloat16)
    mixed = lax.all_gather(mixed_half.reshape(tokens, channels), "tp", axis=0)
    picked = jnp.take(modulation, timestep, axis=0).astype(jnp.float32)
    send = call(
        project_kernel,
        (COLS, tokens + half, LANES),
        mixed,
        picked[:, 0],
        picked[:, 1],
        query_weight,
        key_weight,
        value_weight,
    )
    held = lax.all_to_all(send, "patch", 0, 0, axis_index_groups=Y_GROUPS)
    copies = jnp.broadcast_to(held[None, :, :tokens], (ROWS, COLS, tokens, LANES))
    kv = lax.all_to_all(copies, "patch", 0, 0, axis_index_groups=X_GROUPS)
    result = call(
        attend_kernel,
        (COLS, half, LANES),
        held[:, tokens:],
        kv.reshape(ROWS * COLS * tokens, LANES),
    )
    back = lax.all_to_all(result, "patch", 0, 0, axis_index_groups=Y_GROUPS)
    out = call(unpack_kernel, (frames, half, local_width), back)
    return out.reshape(frames, tile_rows, tile_cols, local_width)


def solution(mesh):
    in_specs = (
        P("frame", "patch", None, "tp"),
        P("frame", "patch", None, "tp"),
        P(),
        P("frame"),
        P(),
        P(None, "tp"),
        P(None, "tp"),
        P(None, "tp"),
    )
    out_specs = P("frame", "patch", None, "tp")
    return jax.shard_map(local, mesh=mesh, in_specs=in_specs, out_specs=out_specs, check_vma=False)
```

```python
import jax
import jax.numpy as jnp
from jax import lax
from jax.experimental import pallas as pl
from jax.experimental.pallas import tpu as pltpu
from jax.sharding import PartitionSpec as P

HEAD_DIM = 64
LANES = 128
ROWS = 4
COLS = 8
LOG2E = 1.4426950408889634
X_GROUPS = [[x * COLS + y for x in range(ROWS)] for y in range(COLS)]
Y_GROUPS = [[x * COLS + y for y in range(COLS)] for x in range(ROWS)]


BLOCK = 64
LEAST = 16


def dequantize_kernel(codes_ref, exponents_ref, *out_refs):
    frames, rows, cols, channels = codes_ref.shape
    groups = exponents_ref.shape[-1]
    tokens = rows * cols
    group = lax.broadcasted_iota(jnp.int32, (groups, channels), 0)
    owner = lax.broadcasted_iota(jnp.int32, (groups, channels), 1) // BLOCK
    spread = (group == owner).astype(jnp.bfloat16)
    for f in range(frames):
        raised = exponents_ref[f].reshape(tokens, groups) + LEAST
        factor = (jnp.left_shift(1, raised).astype(jnp.float32) * 2.0**-LEAST).astype(jnp.bfloat16)
        factor = jnp.dot(factor, spread, preferred_element_type=jnp.float32)
        values = codes_ref[f].reshape(tokens, channels).astype(jnp.float32) * factor
        out_refs[f][...] = values.astype(jnp.bfloat16).reshape(rows, cols, channels)


def shifted_sum(sums):
    before, here, after = sums
    cols = here.shape[0]
    column = lax.broadcasted_iota(jnp.int32, here.shape, 0)
    before = jnp.where(column == 0, 0.0, pltpu.roll(before, 1, 0))
    after = jnp.where(column == cols - 1, 0.0, pltpu.roll(after, cols - 1, 0))
    return before + here + after


def add_taps(sums, slab, weights, a, b):
    for c in range(3):
        tap = (a * 3 + b) * 3 + c
        term = slab * weights[tap : tap + 1]
        sums[c] = term if sums[c] is None else sums[c] + term


def conv_own_kernel(before_ref, first_ref, second_ref, after_ref, weight_ref, out_ref):
    planes = (before_ref, first_ref, second_ref, after_ref)
    rows, cols, channels = first_ref.shape
    for start in range(0, channels, LANES):
        lanes = slice(start, start + LANES)
        weights = weight_ref[:, lanes]
        slabs = [[p[r, :, lanes].astype(jnp.float32) for r in range(rows)] for p in planes]
        for f in range(2):
            for r in range(rows):
                sums = [None] * 3
                for a in range(3):
                    for source in range(rows):
                        add_taps(sums, slabs[f + a][source], weights, a, source - r + 1)
                place = (f * rows + r) * cols
                out_ref[place : place + cols, lanes] = slabs[f + 1][r] + shifted_sum(sums)


def conv_edge_kernel(part_ref, above_ref, below_ref, weight_ref, out_ref):
    planes, cols, channels = above_ref.shape
    for start in range(0, channels, LANES):
        lanes = slice(start, start + LANES)
        weights = weight_ref[:, lanes]
        for r, ref, b in ((0, above_ref, 0), (1, below_ref, 2)):
            slabs = [ref[p, :, lanes].astype(jnp.float32) for p in range(planes)]
            for f in range(2):
                sums = [None] * 3
                for a in range(3):
                    add_taps(sums, slabs[f + a], weights, a, b)
                place = (f * 2 + r) * cols
                total = part_ref[place : place + cols, lanes] + shifted_sum(sums)
                out_ref[place : place + cols, lanes] = total.astype(jnp.bfloat16)


def neighbours(last, first, axis):
    size = lax.axis_size(axis)
    up = [(i, i + 1) for i in range(size - 1)]
    down = [(j, i) for i, j in up]
    return lax.ppermute(last, axis, up), lax.ppermute(first, axis, down)


def low_lanes(shape):
    return lax.broadcasted_iota(jnp.int32, shape, len(shape) - 1) < HEAD_DIM


def swap(x):
    return pltpu.roll(x, HEAD_DIM, x.ndim - 1)


def project_kernel(mixed_ref, shift_ref, scale_ref, wq_ref, wk_ref, wv_ref, out_ref):
    half = mixed_ref.shape[1] // 2
    parts = []
    for f in range(2):
        rows = pl.ds(f * half, half)
        x = jnp.concatenate([mixed_ref[0, rows, :], mixed_ref[1, rows, :]], axis=1)
        x = x.astype(jnp.float32)
        average = jnp.mean(x, axis=1, keepdims=True)
        centered = x - average
        variance = jnp.mean(centered * centered, axis=1, keepdims=True)
        x = centered * lax.rsqrt(variance + 1e-06)
        x = x * (1.0 + scale_ref[f : f + 1, :]) + shift_ref[f : f + 1, :]
        parts.append(x.astype(jnp.bfloat16))
    normed = jnp.concatenate(parts, axis=0)
    tokens = 2 * half
    low_all, low_half = low_lanes((tokens, LANES)), low_lanes((half, LANES))
    q, k, v = [
        jnp.dot(normed, w[...], preferred_element_type=jnp.float32)
        for w in (wq_ref, wk_ref, wv_ref)
    ]
    heads = wq_ref.shape[1] // HEAD_DIM
    for pair in range(heads // 2):
        lanes = slice(pair * LANES, (pair + 1) * LANES)
        qp, kp, vp = q[:, lanes], k[:, lanes], v[:, lanes]
        first, second = qp[:half], qp[half:]
        even, odd = 2 * pair, 2 * pair + 1
        out_ref[even, :tokens, :] = jnp.where(low_all, kp, swap(vp)).astype(jnp.bfloat16)
        out_ref[odd, :tokens, :] = jnp.where(low_all, swap(kp), vp).astype(jnp.bfloat16)
        out_ref[even, tokens:, :] = jnp.where(low_half, first, swap(second)).astype(jnp.bfloat16)
        out_ref[odd, tokens:, :] = jnp.where(low_half, swap(first), second).astype(jnp.bfloat16)
    for slot in range(heads, out_ref.shape[0]):
        out_ref[slot] = jnp.zeros(out_ref.shape[1:], jnp.bfloat16)


def query_rows(held_ref, start, step):
    tokens = held_ref.shape[1] * 2 // 3
    rows = step * (held_ref.shape[1] - tokens)
    packed = held_ref[start : start + step, tokens:, :].reshape(rows, LANES).astype(jnp.float32)
    low = low_lanes((rows, LANES))
    first = jnp.where(low, packed, 0.0)
    second = jnp.where(low, swap(packed), 0.0)
    return jnp.concatenate([first, second], axis=0).astype(jnp.bfloat16)


def scored(queries, kv):
    return lax.dot_general(
        queries, kv, (((1,), (1,)), ((), ())), preferred_element_type=jnp.float32
    )


def counted(kv):
    return jnp.where(low_lanes(kv.shape), jnp.ones_like(kv), kv)


FACTOR = LOG2E * HEAD_DIM ** (-0.5)


def copies_kernel(held_ref, out_ref):
    tokens = out_ref.shape[2]
    kv = held_ref[:, :tokens, :]
    for x in range(out_ref.shape[0]):
        out_ref[x] = kv


def attend_own_kernel(held_ref, top_ref, sum_ref):
    slots, width, _ = held_ref.shape
    tokens = width * 2 // 3
    kv = held_ref[:, :tokens, :].reshape(slots * tokens, LANES)
    values = counted(kv)
    step = slots // 2
    rows = step * tokens
    for start in range(0, slots, step):
        scores = scored(query_rows(held_ref, start, step), kv)
        top = jnp.max(scores, axis=1, keepdims=True)
        weights = jnp.exp2((scores - top) * FACTOR).astype(jnp.bfloat16)
        place = slice(start * tokens, start * tokens + rows)
        top_ref[place, :] = jnp.broadcast_to(top, (rows, LANES))
        sum_ref[place, :] = jnp.dot(weights, values, preferred_element_type=jnp.float32)


def attend_kernel(x_ref, held_ref, kv_ref, top_ref, sum_ref, out_ref):
    slots, width, _ = held_ref.shape
    tokens = width * 2 // 3
    half = tokens // 2
    others = [lax.rem(x_ref[0] + j, ROWS) for j in range(1, ROWS)]
    kv = jnp.concatenate([kv_ref[x].reshape(slots * tokens, LANES) for x in others], axis=0)
    values = counted(kv)
    step = slots // 2
    rows = step * tokens
    low = low_lanes((rows // 2, LANES))
    starts = list(range(0, slots, step))
    scores = scored(query_rows(held_ref, 0, step), kv)
    for start in starts:
        later = None
        if start != starts[-1]:
            later = scored(query_rows(held_ref, start + step, step), kv)
        place = slice(start * tokens, start * tokens + rows)
        own_top = top_ref[place, :][:, :1]
        top = jnp.maximum(jnp.max(scores, axis=1, keepdims=True), own_top)
        weights = jnp.exp2((scores - top) * FACTOR).astype(jnp.bfloat16)
        summed = jnp.dot(weights, values, preferred_element_type=jnp.float32)
        summed = summed + sum_ref[place, :] * jnp.exp2((own_top - top) * FACTOR)
        done = summed / swap(summed)
        result = jnp.where(low, swap(done[: rows // 2]), done[rows // 2 :])
        out_ref[start : start + step] = result.astype(jnp.bfloat16).reshape(step, half, LANES)
        scores = later


def unpack_kernel(in_ref, out_ref):
    half = in_ref.shape[1]
    low = low_lanes((half, LANES))
    for pair in range(out_ref.shape[2] // LANES):
        lanes = slice(pair * LANES, (pair + 1) * LANES)
        even = in_ref[2 * pair].astype(jnp.float32)
        odd = in_ref[2 * pair + 1].astype(jnp.float32)
        out_ref[0, :, lanes] = jnp.where(low, even, swap(odd)).astype(jnp.bfloat16)
        out_ref[1, :, lanes] = jnp.where(low, swap(even), odd).astype(jnp.bfloat16)


def call(kernel, shapes, *args, scalars=0):
    shapes = [jax.ShapeDtypeStruct(shape, kind) for shape, kind in shapes]
    in_specs = [pl.BlockSpec(memory_space=pltpu.SMEM)] * scalars
    in_specs += [pl.BlockSpec(memory_space=pltpu.VMEM)] * (len(args) - scalars)
    return pl.pallas_call(
        kernel,
        out_shape=shapes,
        in_specs=in_specs,
        out_specs=[pl.BlockSpec(memory_space=pltpu.VMEM)] * len(shapes),
        compiler_params=pltpu.CompilerParams(vmem_limit_bytes=48 * 1024 * 1024),
    )(*args)


def local(
    residual_codes,
    exponents,
    conv_weight,
    timestep,
    modulation,
    query_weight,
    key_weight,
    value_weight,
):
    frames, tile_rows, tile_cols, channels = residual_codes.shape
    local_width = query_weight.shape[1]
    tokens = frames * tile_rows * tile_cols
    half = tokens // 2
    narrow, wide = jnp.bfloat16, jnp.float32
    pair_index = lax.axis_index("tp")
    taps = lax.dynamic_slice_in_dim(conv_weight, pair_index * channels, channels, 3)
    taps = taps.reshape(27, channels).astype(wide)
    picked = jnp.take(modulation, timestep, axis=0).astype(wide)

    frame_shape = ((tile_rows, tile_cols, channels), narrow)
    first, second = call(dequantize_kernel, [frame_shape] * 2, residual_codes, exponents)
    before, after = neighbours(second, first, "frame")
    planes = (before, first, second, after)
    top_row = jnp.stack([p[0] for p in planes])
    bottom_row = jnp.stack([p[-1] for p in planes])
    above, below = neighbours(bottom_row, top_row, "patch")
    (part,) = call(conv_own_kernel, [((tokens, channels), wide)], *planes, taps)
    (mixed_half,) = call(
        conv_edge_kernel, [((tokens, channels), narrow)], part, above, below, taps
    )
    mixed = lax.all_gather(mixed_half, "tp", axis=0)
    (send,) = call(
        project_kernel,
        [((COLS, tokens + half, LANES), narrow)],
        mixed,
        picked[:, 0],
        picked[:, 1],
        query_weight,
        key_weight,
        value_weight,
    )
    held = lax.all_to_all(send, "patch", 0, 0, axis_index_groups=Y_GROUPS)
    (copies,) = call(copies_kernel, [((ROWS, COLS, tokens, LANES), narrow)], held)
    kv = lax.all_to_all(copies, "patch", 0, 0, axis_index_groups=X_GROUPS)
    partial = ((COLS * tokens, LANES), wide)
    top, summed = call(attend_own_kernel, [partial] * 2, held)
    x_index = (lax.axis_index("patch") // COLS).reshape(1)
    (result,) = call(
        attend_kernel,
        [((COLS, half, LANES), narrow)],
        x_index,
        held,
        kv,
        top,
        summed,
        scalars=1,
    )
    back = lax.all_to_all(result, "patch", 0, 0, axis_index_groups=Y_GROUPS)
    (out,) = call(unpack_kernel, [((frames, half, local_width), narrow)], back)
    return out.reshape(frames, tile_rows, tile_cols, local_width)


def solution(mesh):
    in_specs = (
        P("frame", "patch", None, "tp"),
        P("frame", "patch", None, "tp"),
        P(),
        P("frame"),
        P(),
        P(None, "tp"),
        P(None, "tp"),
        P(None, "tp"),
    )
    out_specs = P("frame", "patch", None, "tp")
    return jax.shard_map(local, mesh=mesh, in_specs=in_specs, out_specs=out_specs, check_vma=False)
```

```python
import jax
import jax.numpy as jnp
from jax import lax
from jax.experimental import pallas as pl
from jax.experimental.pallas import tpu as pltpu
from jax.sharding import PartitionSpec as P

HEAD_DIM = 64
LANES = 128
ROWS = 4
COLS = 8
LOG2E = 1.4426950408889634
X_GROUPS = [[x * COLS + y for x in range(ROWS)] for y in range(COLS)]
Y_GROUPS = [[x * COLS + y for y in range(COLS)] for x in range(ROWS)]


BLOCK = 64
LEAST = 16


def dequantize_kernel(codes_ref, exponents_ref, first_ref, second_ref, codes, exps, sems):
    frames, rows, cols, channels = codes.shape
    groups = exps.shape[1]
    small = pltpu.make_async_copy(exponents_ref, exps, sems.at[frames * rows])
    small.start()
    copies = []
    for f in range(frames):
        for r in range(rows):
            place = f * rows + r
            copy = pltpu.make_async_copy(codes_ref.at[f, r], codes.at[f, r], sems.at[place])
            copy.start()
            copies.append(copy)
    group = lax.broadcasted_iota(jnp.int32, (groups, channels), 0)
    owner = lax.broadcasted_iota(jnp.int32, (groups, channels), 1) // BLOCK
    spread = (group == owner).astype(jnp.bfloat16)
    small.wait()
    for f, out_ref in enumerate((first_ref, second_ref)):
        for r in range(rows):
            raised = exps[f, :, r, :] + LEAST
            factor = jnp.left_shift(1, raised).astype(jnp.float32) * 2.0**-LEAST
            factor = lax.dot_general(
                factor.astype(jnp.bfloat16),
                spread,
                (((0,), (0,)), ((), ())),
                preferred_element_type=jnp.float32,
            )
            copies[f * rows + r].wait()
            out_ref[r] = (codes[f, r].astype(jnp.float32) * factor).astype(jnp.bfloat16)


def shifted_sum(sums):
    before, here, after = sums
    cols = here.shape[0]
    column = lax.broadcasted_iota(jnp.int32, here.shape, 0)
    before = jnp.where(column == 0, 0.0, pltpu.roll(before, 1, 0))
    after = jnp.where(column == cols - 1, 0.0, pltpu.roll(after, cols - 1, 0))
    return before + here + after


def add_taps(sums, slab, weights, a, b):
    for c in range(3):
        tap = (a * 3 + b) * 3 + c
        term = slab * weights[tap : tap + 1]
        sums[c] = term if sums[c] is None else sums[c] + term


def conv_own_kernel(before_ref, first_ref, second_ref, after_ref, weight_ref, out_ref):
    planes = (before_ref, first_ref, second_ref, after_ref)
    rows, cols, channels = first_ref.shape
    for start in range(0, channels, LANES):
        lanes = slice(start, start + LANES)
        weights = weight_ref[:, lanes]
        slabs = [[p[r, :, lanes].astype(jnp.float32) for r in range(rows)] for p in planes]
        for f in range(2):
            for r in range(rows):
                sums = [None] * 3
                for a in range(3):
                    for source in range(rows):
                        add_taps(sums, slabs[f + a][source], weights, a, source - r + 1)
                place = (f * rows + r) * cols
                out_ref[place : place + cols, lanes] = slabs[f + 1][r] + shifted_sum(sums)


def conv_edge_kernel(part_ref, above_ref, below_ref, weight_ref, out_ref):
    planes, cols, channels = above_ref.shape
    for start in range(0, channels, LANES):
        lanes = slice(start, start + LANES)
        weights = weight_ref[:, lanes]
        for r, ref, b in ((0, above_ref, 0), (1, below_ref, 2)):
            slabs = [ref[p, :, lanes].astype(jnp.float32) for p in range(planes)]
            for f in range(2):
                sums = [None] * 3
                for a in range(3):
                    add_taps(sums, slabs[f + a], weights, a, b)
                place = (f * 2 + r) * cols
                total = part_ref[place : place + cols, lanes] + shifted_sum(sums)
                out_ref[place : place + cols, lanes] = total.astype(jnp.bfloat16)


def neighbours(last, first, axis):
    size = lax.axis_size(axis)
    up = [(i, i + 1) for i in range(size - 1)]
    down = [(j, i) for i, j in up]
    return lax.ppermute(last, axis, up), lax.ppermute(first, axis, down)


def low_lanes(shape):
    return lax.broadcasted_iota(jnp.int32, shape, len(shape) - 1) < HEAD_DIM


def swap(x):
    return pltpu.roll(x, HEAD_DIM, x.ndim - 1)


def project_kernel(step_ref, mixed_ref, modulation_ref, wq_ref, wk_ref, wv_ref, out_ref):
    half = mixed_ref.shape[1] // 2
    parts = []
    for f in range(2):
        rows = pl.ds(f * half, half)
        x = jnp.concatenate([mixed_ref[0, rows, :], mixed_ref[1, rows, :]], axis=1)
        x = x.astype(jnp.float32)
        average = jnp.mean(x, axis=1, keepdims=True)
        centered = x - average
        variance = jnp.mean(centered * centered, axis=1, keepdims=True)
        x = centered * lax.rsqrt(variance + 1e-06)
        picked = modulation_ref[step_ref[f]].astype(jnp.float32)
        x = x * (1.0 + picked[1:2]) + picked[0:1]
        parts.append(x.astype(jnp.bfloat16))
    normed = jnp.concatenate(parts, axis=0)
    tokens = 2 * half
    low_all, low_half = low_lanes((tokens, LANES)), low_lanes((half, LANES))
    q, k, v = [
        jnp.dot(normed, w[...], preferred_element_type=jnp.float32)
        for w in (wq_ref, wk_ref, wv_ref)
    ]
    heads = wq_ref.shape[1] // HEAD_DIM
    for pair in range(heads // 2):
        lanes = slice(pair * LANES, (pair + 1) * LANES)
        qp, kp, vp = q[:, lanes], k[:, lanes], v[:, lanes]
        first, second = qp[:half], qp[half:]
        even, odd = 2 * pair, 2 * pair + 1
        out_ref[even, :tokens, :] = jnp.where(low_all, kp, swap(vp)).astype(jnp.bfloat16)
        out_ref[odd, :tokens, :] = jnp.where(low_all, swap(kp), vp).astype(jnp.bfloat16)
        out_ref[even, tokens:, :] = jnp.where(low_half, first, swap(second)).astype(jnp.bfloat16)
        out_ref[odd, tokens:, :] = jnp.where(low_half, swap(first), second).astype(jnp.bfloat16)
    for slot in range(heads, out_ref.shape[0]):
        out_ref[slot] = jnp.zeros(out_ref.shape[1:], jnp.bfloat16)


def query_rows(held_ref, start, step):
    tokens = held_ref.shape[1] * 2 // 3
    rows = step * (held_ref.shape[1] - tokens)
    packed = held_ref[start : start + step, tokens:, :].reshape(rows, LANES).astype(jnp.float32)
    low = low_lanes((rows, LANES))
    first = jnp.where(low, packed, 0.0)
    second = jnp.where(low, swap(packed), 0.0)
    return jnp.concatenate([first, second], axis=0).astype(jnp.bfloat16)


def scored(queries, kv):
    return lax.dot_general(
        queries, kv, (((1,), (1,)), ((), ())), preferred_element_type=jnp.float32
    )


def counted(kv):
    return jnp.where(low_lanes(kv.shape), jnp.ones_like(kv), kv)


FACTOR = LOG2E * HEAD_DIM ** (-0.5)


def copies_kernel(held_ref, out_ref, sems):
    tokens = out_ref.shape[2]
    copies = [
        pltpu.make_async_copy(held_ref.at[:, pl.ds(0, tokens), :], out_ref.at[x], sems.at[x])
        for x in range(out_ref.shape[0])
    ]
    for copy in copies:
        copy.start()
    for copy in copies:
        copy.wait()


def attend_own_kernel(held_ref, top_ref, sum_ref):
    slots, width, _ = held_ref.shape
    tokens = width * 2 // 3
    kv = held_ref[:, :tokens, :].reshape(slots * tokens, LANES)
    values = counted(kv)
    step = slots // 2
    rows = step * tokens
    for start in range(0, slots, step):
        scores = scored(query_rows(held_ref, start, step), kv)
        top = jnp.max(scores, axis=1, keepdims=True)
        weights = jnp.exp2((scores - top) * FACTOR).astype(jnp.bfloat16)
        place = slice(start * tokens, start * tokens + rows)
        top_ref[place, :] = jnp.broadcast_to(top, (rows, LANES))
        sum_ref[place, :] = jnp.dot(weights, values, preferred_element_type=jnp.float32)


def attend_kernel(x_ref, held_ref, kv_ref, top_ref, sum_ref, out_ref):
    slots, width, _ = held_ref.shape
    tokens = width * 2 // 3
    half = tokens // 2
    others = [lax.rem(x_ref[0] + j, ROWS) for j in range(1, ROWS)]
    kv = jnp.concatenate([kv_ref[x].reshape(slots * tokens, LANES) for x in others], axis=0)
    values = counted(kv)
    step = slots // 2
    rows = step * tokens
    low = low_lanes((rows // 2, LANES))
    starts = list(range(0, slots, step))
    scores = scored(query_rows(held_ref, 0, step), kv)
    for start in starts:
        later = None
        if start != starts[-1]:
            later = scored(query_rows(held_ref, start + step, step), kv)
        place = slice(start * tokens, start * tokens + rows)
        own_top = top_ref[place, :][:, :1]
        top = jnp.maximum(jnp.max(scores, axis=1, keepdims=True), own_top)
        weights = jnp.exp2((scores - top) * FACTOR).astype(jnp.bfloat16)
        summed = jnp.dot(weights, values, preferred_element_type=jnp.float32)
        summed = summed + sum_ref[place, :] * jnp.exp2((own_top - top) * FACTOR)
        done = summed / swap(summed)
        result = jnp.where(low, swap(done[: rows // 2]), done[rows // 2 :])
        out_ref[start : start + step] = result.astype(jnp.bfloat16).reshape(step, half, LANES)
        scores = later


def unpack_kernel(in_ref, out_ref):
    half = in_ref.shape[1]
    low = low_lanes((half, LANES))
    for pair in range(out_ref.shape[2] // LANES):
        lanes = slice(pair * LANES, (pair + 1) * LANES)
        even = in_ref[2 * pair].astype(jnp.float32)
        odd = in_ref[2 * pair + 1].astype(jnp.float32)
        out_ref[0, :, lanes] = jnp.where(low, even, swap(odd)).astype(jnp.bfloat16)
        out_ref[1, :, lanes] = jnp.where(low, swap(even), odd).astype(jnp.bfloat16)


SMEM = pl.BlockSpec(memory_space=pltpu.SMEM)
VMEM = pl.BlockSpec(memory_space=pltpu.VMEM)
HBM = pl.BlockSpec(memory_space=pltpu.HBM)


def call(kernel, shapes, *args, spaces=None, out_space=VMEM, scratch=()):
    shapes = [jax.ShapeDtypeStruct(shape, kind) for shape, kind in shapes]
    return pl.pallas_call(
        kernel,
        out_shape=shapes,
        in_specs=spaces or [VMEM] * len(args),
        out_specs=[out_space] * len(shapes),
        scratch_shapes=scratch,
        compiler_params=pltpu.CompilerParams(vmem_limit_bytes=48 * 1024 * 1024),
    )(*args)


def local(
    residual_codes,
    exponents,
    conv_weight,
    timestep,
    modulation,
    query_weight,
    key_weight,
    value_weight,
):
    frames, tile_rows, tile_cols, channels = residual_codes.shape
    local_width = query_weight.shape[1]
    tokens = frames * tile_rows * tile_cols
    half = tokens // 2
    narrow, wide = jnp.bfloat16, jnp.float32
    pair_index = lax.axis_index("tp")
    taps = lax.dynamic_slice_in_dim(conv_weight, pair_index * channels, channels, 3)
    taps = taps.reshape(27, channels).astype(wide)

    frame_shape = ((tile_rows, tile_cols, channels), narrow)
    by_group = exponents.transpose(0, 3, 1, 2)
    first, second = call(
        dequantize_kernel,
        [frame_shape] * 2,
        pltpu.with_memory_space_constraint(residual_codes, pltpu.HBM),
        pltpu.with_memory_space_constraint(by_group, pltpu.HBM),
        spaces=[HBM, HBM],
        scratch=[
            pltpu.VMEM(residual_codes.shape, jnp.int32),
            pltpu.VMEM(by_group.shape, jnp.int32),
            pltpu.SemaphoreType.DMA((frames * tile_rows + 1,)),
        ],
    )
    before, after = neighbours(second, first, "frame")
    planes = (before, first, second, after)
    top_row = jnp.stack([p[0] for p in planes])
    bottom_row = jnp.stack([p[-1] for p in planes])
    above, below = neighbours(bottom_row, top_row, "patch")
    (part,) = call(conv_own_kernel, [((tokens, channels), wide)], *planes, taps)
    (mixed_half,) = call(
        conv_edge_kernel, [((tokens, channels), narrow)], part, above, below, taps
    )
    mixed = lax.all_gather(mixed_half, "tp", axis=0)
    (send,) = call(
        project_kernel,
        [((COLS, tokens + half, LANES), narrow)],
        timestep,
        mixed,
        modulation,
        query_weight,
        key_weight,
        value_weight,
        spaces=[SMEM] + [VMEM] * 5,
    )
    held = lax.all_to_all(send, "patch", 0, 0, axis_index_groups=Y_GROUPS)
    (copies,) = call(
        copies_kernel,
        [((ROWS, COLS, tokens, LANES), narrow)],
        held,
        out_space=HBM,
        scratch=[pltpu.SemaphoreType.DMA((ROWS,))],
    )
    kv = lax.all_to_all(copies, "patch", 0, 0, axis_index_groups=X_GROUPS)
    partial = ((COLS * tokens, LANES), wide)
    top, summed = call(attend_own_kernel, [partial] * 2, held)
    x_index = (lax.axis_index("patch") // COLS).reshape(1)
    (result,) = call(
        attend_kernel,
        [((COLS, half, LANES), narrow)],
        x_index,
        held,
        kv,
        top,
        summed,
        spaces=[SMEM] + [VMEM] * 4,
    )
    back = lax.all_to_all(result, "patch", 0, 0, axis_index_groups=Y_GROUPS)
    (out,) = call(unpack_kernel, [((frames, half, local_width), narrow)], back)
    return out.reshape(frames, tile_rows, tile_cols, local_width)


def solution(mesh):
    in_specs = (
        P("frame", "patch", None, "tp"),
        P("frame", "patch", None, "tp"),
        P(),
        P("frame"),
        P(),
        P(None, "tp"),
        P(None, "tp"),
        P(None, "tp"),
    )
    out_specs = P("frame", "patch", None, "tp")
    return jax.shard_map(local, mesh=mesh, in_specs=in_specs, out_specs=out_specs, check_vma=False)
```

```python
import jax
import jax.numpy as jnp
from jax import lax
from jax.experimental import pallas as pl
from jax.experimental.pallas import tpu as pltpu
from jax.sharding import PartitionSpec as P

HEAD_DIM = 64
LANES = 128
ROWS, COLS = 4, 8
BLOCKS = (2, 4)
PLACES = (2, 2)
SLOTS = 8
COPIES = 4
FRAMES = 8


LOG2E = 1.4426950408889634


def device_at(frame, block, place):
    x = 2 * block[0] + (place[0] + block[0]) % 2 + frame % 2
    y = 2 * block[1] + place[1] + frame % 2
    return (frame * ROWS + x % ROWS) * COLS + y % COLS


def pairs(sizes):
    return [(i, j) for i in range(sizes[0]) for j in range(sizes[1])]


HEAD_GROUPS = [
    [device_at(f, block, place) for block in pairs(BLOCKS)]
    for f in range(FRAMES)
    for place in pairs(PLACES)
]
KEY_GROUPS = [
    [device_at(f, block, place) for place in pairs(PLACES)]
    for f in range(FRAMES)
    for block in pairs(BLOCKS)
]


def exchange(x, groups):
    return lax.all_to_all(x, ("frame", "patch"), 0, 0, axis_index_groups=groups)


BLOCK = 64
LEAST = 16


def dequantize_kernel(codes_ref, exponents_ref, first_ref, second_ref, codes, exps, sems):
    frames, rows, cols, channels = codes.shape
    groups = exps.shape[1]
    small = pltpu.make_async_copy(exponents_ref, exps, sems.at[frames * rows])
    small.start()
    copies = []
    for f in range(frames):
        for r in range(rows):
            place = f * rows + r
            copy = pltpu.make_async_copy(codes_ref.at[f, r], codes.at[f, r], sems.at[place])
            copy.start()
            copies.append(copy)
    group = lax.broadcasted_iota(jnp.int32, (groups, channels), 0)
    owner = lax.broadcasted_iota(jnp.int32, (groups, channels), 1) // BLOCK
    spread = (group == owner).astype(jnp.bfloat16)
    small.wait()
    for f, out_ref in enumerate((first_ref, second_ref)):
        for r in range(rows):
            raised = exps[f, :, r, :] + LEAST
            factor = jnp.left_shift(1, raised).astype(jnp.float32) * 2.0**-LEAST
            factor = lax.dot_general(
                factor.astype(jnp.bfloat16),
                spread,
                (((0,), (0,)), ((), ())),
                preferred_element_type=jnp.float32,
            )
            copies[f * rows + r].wait()
            out_ref[r] = (codes[f, r].astype(jnp.float32) * factor).astype(jnp.bfloat16)


def shifted_sum(sums):
    before, here, after = sums
    cols = here.shape[0]
    column = lax.broadcasted_iota(jnp.int32, here.shape, 0)
    before = jnp.where(column == 0, 0.0, pltpu.roll(before, 1, 0))
    after = jnp.where(column == cols - 1, 0.0, pltpu.roll(after, cols - 1, 0))
    return before + here + after


def add_taps(sums, slab, weights, a, b):
    for c in range(3):
        tap = (a * 3 + b) * 3 + c
        term = slab * weights[tap : tap + 1]
        sums[c] = term if sums[c] is None else sums[c] + term


def conv_own_kernel(before_ref, first_ref, second_ref, after_ref, weight_ref, out_ref):
    planes = (before_ref, first_ref, second_ref, after_ref)
    rows, cols, channels = first_ref.shape
    for start in range(0, channels, LANES):
        lanes = slice(start, start + LANES)
        weights = weight_ref[:, lanes]
        slabs = [[p[r, :, lanes].astype(jnp.float32) for r in range(rows)] for p in planes]
        for f in range(2):
            for r in range(rows):
                sums = [None] * 3
                for a in range(3):
                    for source in range(rows):
                        add_taps(sums, slabs[f + a][source], weights, a, source - r + 1)
                place = (f * rows + r) * cols
                out_ref[place : place + cols, lanes] = slabs[f + 1][r] + shifted_sum(sums)


def conv_edge_kernel(part_ref, above_ref, below_ref, weight_ref, out_ref):
    planes, cols, channels = above_ref.shape
    for start in range(0, channels, LANES):
        lanes = slice(start, start + LANES)
        weights = weight_ref[:, lanes]
        for r, ref, b in ((0, above_ref, 0), (1, below_ref, 2)):
            slabs = [ref[p, :, lanes].astype(jnp.float32) for p in range(planes)]
            for f in range(2):
                sums = [None] * 3
                for a in range(3):
                    add_taps(sums, slabs[f + a], weights, a, b)
                place = (f * 2 + r) * cols
                total = part_ref[place : place + cols, lanes] + shifted_sum(sums)
                out_ref[place : place + cols, lanes] = total.astype(jnp.bfloat16)


def neighbours(last, first, axis):
    size = lax.axis_size(axis)
    up = [(i, i + 1) for i in range(size - 1)]
    down = [(j, i) for i, j in up]
    return lax.ppermute(last, axis, up), lax.ppermute(first, axis, down)


def low_lanes(shape):
    return lax.broadcasted_iota(jnp.int32, shape, len(shape) - 1) < HEAD_DIM


def swap(x):
    return pltpu.roll(x, HEAD_DIM, x.ndim - 1)


def pick_kernel(step_ref, modulation_ref, shift_ref, scale_ref):
    for f in range(shift_ref.shape[0]):
        picked = modulation_ref[step_ref[f]].astype(jnp.float32)
        shift_ref[f : f + 1, :] = picked[0:1]
        scale_ref[f : f + 1, :] = picked[1:2]


def project_kernel(mixed_ref, shift_ref, scale_ref, wq_ref, wk_ref, wv_ref, out_ref):
    half = mixed_ref.shape[1] // 2
    parts = []
    for f in range(2):
        rows = pl.ds(f * half, half)
        x = jnp.concatenate([mixed_ref[0, rows, :], mixed_ref[1, rows, :]], axis=1)
        x = x.astype(jnp.float32)
        average = jnp.mean(x, axis=1, keepdims=True)
        centered = x - average
        variance = jnp.mean(centered * centered, axis=1, keepdims=True)
        x = centered * lax.rsqrt(variance + 1e-06)
        x = x * (1.0 + scale_ref[f : f + 1, :]) + shift_ref[f : f + 1, :]
        parts.append(x.astype(jnp.bfloat16))
    normed = jnp.concatenate(parts, axis=0)
    tokens = 2 * half
    low_all, low_half = low_lanes((tokens, LANES)), low_lanes((half, LANES))
    q, k, v = [
        jnp.dot(normed, w[...], preferred_element_type=jnp.float32)
        for w in (wq_ref, wk_ref, wv_ref)
    ]
    heads = wq_ref.shape[1] // HEAD_DIM
    for pair in range(heads // 2):
        lanes = slice(pair * LANES, (pair + 1) * LANES)
        qp, kp, vp = q[:, lanes], k[:, lanes], v[:, lanes]
        first, second = qp[:half], qp[half:]
        even, odd = 2 * pair, 2 * pair + 1
        out_ref[even, :tokens, :] = jnp.where(low_all, kp, swap(vp)).astype(jnp.bfloat16)
        out_ref[odd, :tokens, :] = jnp.where(low_all, swap(kp), vp).astype(jnp.bfloat16)
        out_ref[even, tokens:, :] = jnp.where(low_half, first, swap(second)).astype(jnp.bfloat16)
        out_ref[odd, tokens:, :] = jnp.where(low_half, swap(first), second).astype(jnp.bfloat16)
    for slot in range(heads, out_ref.shape[0]):
        out_ref[slot] = jnp.zeros(out_ref.shape[1:], jnp.bfloat16)


def query_rows(held_ref, start, step):
    tokens = held_ref.shape[1] * 2 // 3
    rows = step * (held_ref.shape[1] - tokens)
    packed = held_ref[start : start + step, tokens:, :].reshape(rows, LANES).astype(jnp.float32)
    low = low_lanes((rows, LANES))
    first = jnp.where(low, packed, 0.0)
    second = jnp.where(low, swap(packed), 0.0)
    return jnp.concatenate([first, second], axis=0).astype(jnp.bfloat16)


def scored(queries, kv):
    return lax.dot_general(
        queries, kv, (((1,), (1,)), ((), ())), preferred_element_type=jnp.float32
    )


def counted(kv):
    return jnp.where(low_lanes(kv.shape), jnp.ones_like(kv), kv)


FACTOR = LOG2E * HEAD_DIM ** (-0.5)


def copies_kernel(held_ref, out_ref):
    tokens = out_ref.shape[2]
    kv = held_ref[:, :tokens, :]
    for x in range(out_ref.shape[0]):
        out_ref[x] = kv


def attend_kernel(held_ref, kv_ref, out_ref):
    slots, half, _ = out_ref.shape
    kv = kv_ref[...].reshape(-1, LANES)
    values = counted(kv)
    step = slots // 2
    low = low_lanes((step * half, LANES))
    starts = list(range(0, slots, step))
    scores = scored(query_rows(held_ref, 0, step), kv)
    for start in starts:
        later = None
        if start != starts[-1]:
            later = scored(query_rows(held_ref, start + step, step), kv)
        top = jnp.max(scores, axis=1, keepdims=True)
        weights = jnp.exp2((scores - top) * FACTOR).astype(jnp.bfloat16)
        summed = jnp.dot(weights, values, preferred_element_type=jnp.float32)
        done = summed / swap(summed)
        result = jnp.where(low, swap(done[: step * half]), done[step * half :])
        out_ref[start : start + step] = result.astype(jnp.bfloat16).reshape(step, half, LANES)
        scores = later


def unpack_kernel(in_ref, out_ref):
    half = in_ref.shape[1]
    low = low_lanes((half, LANES))
    for pair in range(out_ref.shape[2] // LANES):
        lanes = slice(pair * LANES, (pair + 1) * LANES)
        even = in_ref[2 * pair].astype(jnp.float32)
        odd = in_ref[2 * pair + 1].astype(jnp.float32)
        out_ref[0, :, lanes] = jnp.where(low, even, swap(odd)).astype(jnp.bfloat16)
        out_ref[1, :, lanes] = jnp.where(low, swap(even), odd).astype(jnp.bfloat16)


SMEM = pl.BlockSpec(memory_space=pltpu.SMEM)
VMEM = pl.BlockSpec(memory_space=pltpu.VMEM)
HBM = pl.BlockSpec(memory_space=pltpu.HBM)


def call(kernel, shapes, *args, spaces=None, scratch=()):
    shapes = [jax.ShapeDtypeStruct(shape, kind) for shape, kind in shapes]
    return pl.pallas_call(
        kernel,
        out_shape=shapes,
        in_specs=spaces or [VMEM] * len(args),
        out_specs=[VMEM] * len(shapes),
        scratch_shapes=scratch,
        compiler_params=pltpu.CompilerParams(vmem_limit_bytes=48 * 1024 * 1024),
    )(*args)


def local(
    residual_codes,
    exponents,
    conv_weight,
    timestep,
    modulation,
    query_weight,
    key_weight,
    value_weight,
):
    frames, tile_rows, tile_cols, channels = residual_codes.shape
    local_width = query_weight.shape[1]
    tokens = frames * tile_rows * tile_cols
    half = tokens // 2
    narrow, wide = jnp.bfloat16, jnp.float32
    pair_index = lax.axis_index("tp")
    taps = lax.dynamic_slice_in_dim(conv_weight, pair_index * channels, channels, 3)
    taps = taps.reshape(27, channels).astype(wide)
    shift, scale = call(
        pick_kernel,
        [((frames, modulation.shape[2]), wide)] * 2,
        timestep,
        modulation,
        spaces=[SMEM, VMEM],
    )

    frame_shape = ((tile_rows, tile_cols, channels), narrow)
    by_group = exponents.transpose(0, 3, 1, 2)
    first, second = call(
        dequantize_kernel,
        [frame_shape] * 2,
        pltpu.with_memory_space_constraint(residual_codes, pltpu.HBM),
        pltpu.with_memory_space_constraint(by_group, pltpu.HBM),
        spaces=[HBM, HBM],
        scratch=[
            pltpu.VMEM(residual_codes.shape, jnp.int32),
            pltpu.VMEM(by_group.shape, jnp.int32),
            pltpu.SemaphoreType.DMA((frames * tile_rows + 1,)),
        ],
    )
    before, after = neighbours(second, first, "frame")
    planes = (before, first, second, after)
    top_row = jnp.stack([p[0] for p in planes])
    bottom_row = jnp.stack([p[-1] for p in planes])
    above, below = neighbours(bottom_row, top_row, "patch")
    (part,) = call(conv_own_kernel, [((tokens, channels), wide)], *planes, taps)
    (mixed_half,) = call(
        conv_edge_kernel, [((tokens, channels), narrow)], part, above, below, taps
    )
    mixed = lax.all_gather(mixed_half, "tp", axis=0)
    (send,) = call(
        project_kernel,
        [((SLOTS, tokens + half, LANES), narrow)],
        mixed,
        shift,
        scale,
        query_weight,
        key_weight,
        value_weight,
    )
    held = exchange(send, HEAD_GROUPS)
    (copies,) = call(copies_kernel, [((COPIES, SLOTS, tokens, LANES), narrow)], held)
    kv = exchange(copies, KEY_GROUPS)
    (result,) = call(attend_kernel, [((SLOTS, half, LANES), narrow)], held, kv)
    back = exchange(result, HEAD_GROUPS)
    (out,) = call(unpack_kernel, [((frames, half, local_width), narrow)], back)
    return out.reshape(frames, tile_rows, tile_cols, local_width)


def solution(mesh):
    in_specs = (
        P("frame", "patch", None, "tp"),
        P("frame", "patch", None, "tp"),
        P(),
        P("frame"),
        P(),
        P(None, "tp"),
        P(None, "tp"),
        P(None, "tp"),
    )
    out_specs = P("frame", "patch", None, "tp")
    return jax.shard_map(local, mesh=mesh, in_specs=in_specs, out_specs=out_specs, check_vma=False)
```
